32 devices in a mesh: groups: 1, ep: 32 (over z, y, x, core).
Axes of the slice: x: 2, y: 2, z: 4, core: 2. Of those that a mesh axis runs over, the one named last changes fastest.
Arguments:
- cache_src: bfloat16 [32, 1, 32, 32, 576], P(('groups', 'ep')), may hold values from -6 to 6
- lengths: int32 [32], P('groups'), may hold values from 1 to 1024, 16384 in all
- placement: int32 [32], P('groups'), may hold values from 0 to 31, each once
- queries: bfloat16 [256, 64, 576], P(('groups', 'ep')), may hold values from -19 to 19
- new_keys: bfloat16 [256, 576], P(('groups', 'ep')), may hold values from -6 to 6
- hidden: bfloat16 [256, 7168], P(('groups', 'ep')), may hold values from -3 to 3
- latent_value_weight: bfloat16 [64, 512, 128], P('ep'), may hold values from -0.25 to 0.25
- out_weight: bfloat16 [8192, 7168], P('ep'), may hold values from -0.25 to 0.25
- norm_gain: float32 [7168], replicated, may hold values from 0.5 to 1.5
- router: bfloat16 [4, 7168], replicated, may hold values from -0.0625 to 0.0625
- expert_picks: int32 [256, 2], P(('groups', 'ep')), may hold values from 0 to 3, all different within a row; in each aligned block of 8 rows (0 to 7, 8 to 15, ...) at most 8 rows name the same one
- gate_weight: bfloat16 [7168, 4096], P(None, 'ep'), may hold values from -0.0625 to 0.0625
- up_weight: bfloat16 [7168, 4096], P(None, 'ep'), may hold values from -0.0625 to 0.0625
- down_weight: bfloat16 [4096, 7168], P('ep'), may hold values from -0.1875 to 0.1875
Outputs:
- layer_out: bfloat16 [256, 7168], P(('groups', 'ep'))
The draws below stay inside these ranges and needn't reach their ends.
Inputs may be any that keep to these rules, and one draw needn't show every extreme that they name: One request has exactly 1024 live positions; the lengths sum to 16384. `placement`: a permutation: each decode device serves exactly one request. `expert_picks`: the 2 picks of a row differ; among the rows of one device no expert is named more than 8 times, and in some device's rows one expert is named exactly 8 times.
All inputs are finite; a program needn't handle non-finite values.
Results may differ from the reference program's by a relative error of at most 0.015.
Values may be sent and summed in bfloat16 or wider, within the bound.
A program may use at most 64 MiB of HBM per device.

```python
import math
import jax
import jax.numpy as jnp
import numpy as np
from jax import lax

D = 7168
KVL = 512
ROPE = 64
VALUE_HEAD_WIDTH = 128
LOCAL_HEADS = 64
FF = 1024
SPLIT = 8
TOPW = 2
BLK = 32
ROWS_DEV = 8
JB = 1
SOURCES = 32
REQUESTS = 32
LMAX = 1024
DECODE_ROWS = 256
EXPERTS = 4
CAP = 8


def draw_cache_src(key, part):
    key = jax.random.fold_in(key, 11)
    array_shape = (SOURCES, JB, REQUESTS, BLK, KVL + ROPE)
    drawn = jnp.clip(jax.random.normal(key, array_shape, jnp.float32), -6.0, 6.0)
    return drawn.astype(jnp.bfloat16)


def draw_new_keys(key, part):
    key = jax.random.fold_in(key, 12)
    drawn = jnp.clip(jax.random.normal(key, (DECODE_ROWS, KVL + ROPE), jnp.float32), -6.0, 6.0)
    return drawn.astype(jnp.bfloat16)


def draw_queries(key, part):
    key = jax.random.fold_in(key, 13)
    array_shape = (DECODE_ROWS, LOCAL_HEADS, KVL + ROPE)
    drawn = jnp.clip(jax.random.normal(key, array_shape, jnp.float32), -6.0, 6.0)
    return drawn.astype(jnp.bfloat16)


def block_scale(rng, extent, shards, smallest, high):
    def one(axis_at, parts):
        draws = jax.random.uniform(jax.random.fold_in(jax.random.fold_in(rng, 6), axis_at), (parts,), jnp.float32, smallest / len(shards), high / len(shards))
        return jnp.repeat(jnp.exp(draws), extent[axis_at] // parts).reshape((-1,) + (1,) * (len(extent) - axis_at - 1))

    factor_of = one(*shards[0])
    for cut in shards[1:]:
        factor_of = factor_of * one(*cut)
    return factor_of


def length_profile(count, total, bound, slope):
    weights = [(1 << 20) // math.isqrt(grade ** slope) + 1 for grade in range(2, count + 1)]
    spare, counts = total - bound - (count - 1), [1] * (count - 1)
    while spare > 0:
        movable = [i for i in range(count - 1) if counts[i] < bound]
        mass, remaining = sum([weights[i] for i in movable]), spare
        for i in movable:
            more = min(bound - counts[i], max(1, remaining * weights[i] // mass), spare)
            counts[i] = counts[i] + more
            spare = spare - more
    return np.array([bound] + counts)


def ragged(key, count, total, bound, skew):
    if count == 2:
        one = jax.random.randint(key, (), max(1, total - bound), min(bound, total - 1) + 1)
        return jnp.stack([one, total - one])
    sizes = jnp.asarray(length_profile(count, total, bound, skew), jnp.int32)
    pairs = (count - 1) // 2
    source_of, receiver = sizes[1:1 + 2 * pairs:2], sizes[2:2 + 2 * pairs:2]
    room = jnp.minimum(source_of - 1, bound - receiver)
    passed = jax.random.randint(jax.random.fold_in(key, 1), (pairs,), 0, 1 << 20) % (room + 1)
    sizes = sizes.at[1:1 + 2 * pairs:2].set(source_of - passed).at[2:2 + 2 * pairs:2].set(receiver + passed)
    return sizes[jax.random.permutation(jax.random.fold_in(key, 2), count)]


def routed_block(key, own, number, rows, count, top, most, lean):
    sequence = jax.random.permutation(key, count)
    crowded, ordinary = portions_of(count, rows * top, most, lean, True), portions_of(count, rows * top, most, lean, False)
    places = jnp.arange(count)

    def named(sizes, rotation):
        used = int((sizes > 0).sum())
        fixed = max(1, used // 4)
        moved = fixed + (places - fixed + rotation * (used - fixed)) % max(1, count - fixed)
        return jnp.zeros((count,), jnp.int32).at[sequence[jnp.where(places < fixed, places, moved)]].set(jnp.asarray(sizes, jnp.int32))

    sizes = jnp.where(number % 4 == 0, named(crowded, number // 4), named(ordinary, number - number // 4 - 1))
    mixed = jax.random.permutation(jax.random.fold_in(own, 3), count)
    giver, receiver = mixed[0:count // 2 * 2:2], mixed[1:count // 2 * 2:2]
    slack = jnp.minimum(sizes[giver] - 1, most - sizes[receiver]) // 2
    slack = jnp.where((giver == sequence[0]) | (receiver == sequence[0]) | (sizes[receiver] == 0), 0, jnp.maximum(slack, 0))
    moved = jax.random.randint(jax.random.fold_in(own, 4), (count // 2,), 0, 1 << 20) % (slack + 1)
    sizes = sizes.at[giver].add(-moved).at[receiver].add(moved)
    items = jnp.searchsorted(jnp.cumsum(sizes), jnp.arange(rows * top), side="right").astype(jnp.int32)
    table = items.reshape(top, rows).T
    table = table[jax.random.permutation(jax.random.fold_in(own, 1), rows)]
    rotation = jax.random.randint(jax.random.fold_in(own, 2), (rows, 1), 0, top)
    return jnp.take_along_axis(table, (jnp.arange(top)[None, :] + rotation) % top, axis=1)


def portions_of(amount, total, limit, slope, full):
    weights = [(1 << 20) // math.isqrt(standing ** slope) + 1 for standing in range(1, amount + 1)]
    largest = limit if full else min(limit, max(-(-total // amount), total * weights[0] // sum(weights)))
    least = 1 if total - largest >= amount - 1 else 0
    holding, spare = [largest] + [least] * (amount - 1), total - largest - least * (amount - 1)
    while spare > 0:
        candidates = [i for i in range(1, amount) if holding[i] < largest] or [i for i in range(1, amount) if holding[i] < limit]
        whole, left = sum([weights[i] for i in candidates]), spare
        for i in candidates:
            more = min(limit - holding[i], max(1, left * weights[i] // whole), spare)
            holding[i] = holding[i] + more
            spare = spare - more
    return np.array(holding)


def noise(rng, shape, spread, reach, cuts=(), kind=jnp.bfloat16):
    array = jax.random.normal(rng, shape, jnp.float32) * spread
    if len(cuts) > 0:
        array = block_scale(rng, shape, cuts, -0.22, 0.18) * array
    return jnp.clip(array, min=-reach, max=reach).astype(kind)


def setup_inputs(seed: int = 0, part: int = 0) -> dict:
    key_of = jax.random.split(jax.random.key(seed), 15)
    own_keys = jax.random.split(jax.random.fold_in(key_of[14], part), 15)
    cache_src = draw_cache_src(jax.random.fold_in(jax.random.fold_in(key_of[14], part), 71), part)
    lengths = ragged(own_keys[1], REQUESTS, REQUESTS * LMAX // 2, LMAX, 2).astype(jnp.int32)
    placement = jax.random.permutation(own_keys[2], REQUESTS).astype(jnp.int32)
    queries = draw_queries(jax.random.fold_in(jax.random.fold_in(key_of[14], part), 71), part)
    new_keys = draw_new_keys(jax.random.fold_in(jax.random.fold_in(key_of[14], part), 71), part)
    hidden = noise(own_keys[5], (DECODE_ROWS, D), 0.5, 3.0, ((0, 32),))
    latent_value_weight = noise(key_of[6], (LOCAL_HEADS, KVL, VALUE_HEAD_WIDTH), KVL ** -0.5, 0.25, ((0, 32),))
    out_weight = noise(key_of[7], (LOCAL_HEADS * VALUE_HEAD_WIDTH, D), (LOCAL_HEADS * VALUE_HEAD_WIDTH // 16) ** -0.5, 0.25, ((0, 32),))
    norm_gain = jnp.clip(jax.random.uniform(key_of[8], (D,), jnp.float32, 0.5, 1.5), 0.5, 1.5)
    router = noise(key_of[9], (EXPERTS, D), D ** -0.5, 0.0625)
    expert_picks_keys = jax.random.split(jax.random.fold_in(own_keys[10], 1), DECODE_ROWS // ROWS_DEV)
    expert_picks_turns = jax.random.permutation(jax.random.fold_in(own_keys[10], 3), DECODE_ROWS // ROWS_DEV)
    expert_picks = jax.vmap(lambda own, number: routed_block(jax.random.fold_in(own_keys[10], 2), own, number, ROWS_DEV, EXPERTS, TOPW, CAP, 2))(expert_picks_keys, expert_picks_turns).reshape((DECODE_ROWS, TOPW))
    gate_weight = noise(key_of[11], (D, EXPERTS * FF), D ** -0.5, 0.0625, ((1, 32),))
    up_weight = noise(key_of[12], (D, EXPERTS * FF), D ** -0.5, 0.0625, ((1, 32),))
    down_weight = noise(key_of[13], (EXPERTS * FF, D), FF ** -0.5, 0.1875, ((0, 32),))
    return {"cache_src": cache_src, "lengths": lengths, "placement": placement, "queries": queries, "new_keys": new_keys, "hidden": hidden, "latent_value_weight": latent_value_weight, "out_weight": out_weight, "norm_gain": norm_gain, "router": router, "expert_picks": expert_picks, "gate_weight": gate_weight, "up_weight": up_weight, "down_weight": down_weight}


SCORE_SCALE = 192.0 ** (-0.5)
ROUTE_SCALE = 2.5

def reference(cache_src, lengths, placement, queries, new_keys, hidden, latent_value_weight, out_weight, norm_gain, router, expert_picks, gate_weight, up_weight, down_weight):
    request_ids = jnp.arange(REQUESTS, dtype=jnp.int32)
    inverse = lax.optimization_barrier(jnp.sum(jnp.where(placement[None, :] == request_ids[:, None], request_ids[None, :], 0), axis=1)).astype(jnp.int32)
    positions = jnp.arange(LMAX, dtype=jnp.int32)
    cache_width = KVL + ROPE

    def attend(device):
        request = inverse[device]
        column = lax.dynamic_index_in_dim(cache_src, request, 2, keepdims=False)
        key_rows = jnp.transpose(column, (1, 0, 2, 3)).reshape(LMAX, cache_width)
        query_block = lax.dynamic_slice_in_dim(queries, device * ROWS_DEV, ROWS_DEV, 0)
        own_key = lax.dynamic_slice_in_dim(new_keys, device * ROWS_DEV, ROWS_DEV, 0)
        query_rows = query_block.reshape(ROWS_DEV * LOCAL_HEADS, cache_width)
        scores = jnp.dot(query_rows, key_rows.T, preferred_element_type=jnp.float32) * SCORE_SCALE
        scores = jnp.where((positions < lengths[request])[None, :], scores, -jnp.inf)
        own_score = jnp.einsum('rhc,rc->rh', query_block.astype(jnp.float32), own_key.astype(jnp.float32)).reshape(-1) * SCORE_SCALE
        row_top = jnp.maximum(lax.optimization_barrier(jnp.max(scores, axis=1)), own_score)
        weights = jnp.exp(scores - row_top[:, None]).astype(jnp.bfloat16)
        own_weight = lax.optimization_barrier(jnp.exp(own_score - row_top).astype(jnp.bfloat16)).astype(jnp.float32)
        row_total = lax.optimization_barrier(jnp.sum(weights.astype(jnp.float32), axis=1)) + own_weight
        own_values = jnp.broadcast_to(own_key[:, None, :KVL].astype(jnp.float32), (ROWS_DEV, LOCAL_HEADS, KVL)).reshape(-1, KVL)
        summed = jnp.dot(weights, key_rows[:, :KVL], preferred_element_type=jnp.float32) + own_weight[:, None] * own_values
        return (summed / row_total[:, None]).astype(jnp.bfloat16).reshape(ROWS_DEV, LOCAL_HEADS, KVL)
    head_context = lax.map(attend, request_ids).reshape(DECODE_ROWS, LOCAL_HEADS, KVL)
    mixed_values = jnp.einsum('zwn,wns->zws', head_context.astype(jnp.float32), latent_value_weight.astype(jnp.float32)).astype(jnp.bfloat16).reshape(DECODE_ROWS, LOCAL_HEADS * VALUE_HEAD_WIDTH)
    state_rows = hidden.astype(jnp.float32) + jnp.dot(mixed_values, out_weight, preferred_element_type=jnp.float32)
    normed = (state_rows * lax.rsqrt(lax.optimization_barrier(jnp.mean(state_rows * state_rows, axis=1, keepdims=True)) + 1e-06) * norm_gain.astype(jnp.float32)).astype(jnp.bfloat16)
    logits = jnp.dot(normed, router.T, preferred_element_type=jnp.float32)
    gate_score = jax.nn.sigmoid(jnp.take_along_axis(logits, expert_picks, axis=1))
    route_share = ROUTE_SCALE * gate_score / lax.optimization_barrier(jnp.sum(gate_score, axis=1, keepdims=True))
    slice_units = FF // SPLIT

    def expert(moe_sum, expert_id):
        gate_rows = jnp.dot(normed, lax.dynamic_slice_in_dim(gate_weight, expert_id * FF, FF, 1), preferred_element_type=jnp.float32)
        up_rows = jnp.dot(normed, lax.dynamic_slice_in_dim(up_weight, expert_id * FF, FF, 1), preferred_element_type=jnp.float32)
        activated = (jax.nn.silu(gate_rows) * up_rows).astype(jnp.bfloat16).reshape(DECODE_ROWS, SPLIT, slice_units)
        down_slices = lax.dynamic_slice_in_dim(down_weight, expert_id * FF, FF, 0).reshape(SPLIT, slice_units, D)
        slice_out = jnp.einsum('rkf,kfd->krd', activated.astype(jnp.float32), down_slices.astype(jnp.float32)).astype(jnp.bfloat16)
        expert_out = lax.optimization_barrier(jnp.sum(slice_out.astype(jnp.float32), axis=0))
        weight_rows = lax.optimization_barrier(jnp.sum(jnp.where(expert_picks == expert_id, route_share, 0.0), axis=1))
        return (moe_sum + weight_rows[:, None] * expert_out, None)
    moe_sum, unused = lax.scan(expert, jnp.zeros((DECODE_ROWS, D), jnp.float32), jnp.arange(EXPERTS, dtype=jnp.int32))
    return (state_rows + moe_sum).astype(jnp.bfloat16)
```

```python
import functools

import jax
import jax.numpy as jnp
from jax import lax
from jax.experimental import pallas as pl
from jax.experimental.pallas import tpu as pltpu
from jax.sharding import PartitionSpec as P

SPLIT = 8
SCORE_SCALE = 192.0 ** (-0.5)
ROUTE_SCALE = 2.5
TILE = 256
F32 = jnp.float32
BF16 = jnp.bfloat16
NT = (((1,), (1,)), ((), ()))


def dims_of(mesh):
    n = mesh.shape["ep"]
    if mesh.shape["groups"] == 1 and n % 8 == 0:
        return (n // 8, 2, 2, 2)
    return (n // 2, 2)


def orders_of(dims):
    if len(dims) == 4:
        return ((3, 2, 1, 0), (3, 1, 2, 0))
    return ((1, 0), (1, 0))


def strides_of(dims):
    out, step = [], 1
    for size in reversed(dims):
        out.append(step)
        step *= size
    return tuple(reversed(out))


def place_of(flat, dims):
    out = []
    for size in reversed(dims):
        out.append(lax.rem(flat, size))
        flat = lax.div(flat, size)
    return tuple(reversed(out))


def remote(src, dst, send, recv, target):
    return pltpu.make_async_remote_copy(
        src_ref=src,
        dst_ref=dst,
        send_sem=send,
        recv_sem=recv,
        device_id={"ep": target},
        device_id_type=pl.DeviceIdType.MESH,
    )


def attend_kernel(
    n,
    inverse,
    length,
    cache,
    queries,
    new_keys,
    value_weight,
    mixed,
    staged,
    keys,
    by_head,
    context,
    gathered,
    key_send,
    key_recv,
    ctx_send,
    ctx_recv,
):
    me = lax.axis_index("ep")
    rows, latent = new_keys.shape[0], value_weight.shape[1]
    total_rows = queries.shape[0]
    heads = total_rows // rows
    held = value_weight.shape[0]
    chunk = held * rows
    span = keys.shape[1]
    barrier = pltpu.get_barrier_semaphore()

    def greet(k, carry):
        pl.semaphore_signal(
            barrier,
            inc=1,
            device_id={"ep": lax.rem(me + k, n)},
            device_id_type=pl.DeviceIdType.MESH,
        )
        return carry

    lax.fori_loop(1, n, greet, 0)
    pl.semaphore_wait(barrier, n - 1)

    def send_keys(k, carry):
        peer = lax.rem(me + k, n)
        staged[peer] = cache[inverse[peer]]
        remote(staged.at[peer], keys.at[me], key_send, key_recv, peer).start()
        return carry

    lax.fori_loop(1, n, send_keys, 0)
    keys[me] = cache[inverse[me]]

    to = lax.broadcasted_iota(jnp.int32, (total_rows, total_rows), 0)
    source = lax.broadcasted_iota(jnp.int32, (total_rows, total_rows), 1)
    moved = (lax.rem(to, rows) * heads + lax.div(to, rows) == source).astype(BF16)
    by_head[...] = jnp.dot(moved, queries[...], preferred_element_type=F32).astype(BF16)

    wait_rest = pltpu.make_async_copy(keys.at[pl.ds(0, n - 1)], keys.at[pl.ds(0, n - 1)], key_recv)
    wait_rest.wait()
    pltpu.make_async_copy(staged.at[pl.ds(0, n - 1)], staged.at[pl.ds(0, n - 1)], key_send).wait()

    block = min(total_rows, 128)
    blocks = total_rows // block
    per_block = block // chunk
    live = length[0]
    first = lax.div(me, per_block)

    def attend(step, carry):
        at = lax.rem(first + 1 + step, blocks)
        begin = pl.multiple_of(at * block, block)
        q = by_head[pl.ds(begin, block), :]
        key_rows = keys[...].reshape(n * span, keys.shape[2])
        own_keys = new_keys[...].astype(F32)
        spread = jnp.broadcast_to(own_keys[None], (block // rows,) + own_keys.shape)
        spread = spread.reshape(block, own_keys.shape[1])
        own = jnp.sum(q.astype(F32) * spread, axis=1, keepdims=True) * SCORE_SCALE
        scores = lax.dot_general(q, key_rows, NT, preferred_element_type=F32) * SCORE_SCALE
        position = lax.broadcasted_iota(jnp.int32, scores.shape, 1)
        scores = jnp.where(position < live, scores, -jnp.inf)
        top = jnp.maximum(jnp.max(scores, axis=1, keepdims=True), own)
        weights = jnp.exp(scores - top).astype(BF16)
        own_weight = jnp.exp(own - top).astype(BF16).astype(F32)
        whole = jnp.sum(weights.astype(F32), axis=1, keepdims=True) + own_weight
        summed = jnp.dot(weights, key_rows[:, :latent], preferred_element_type=F32)
        summed = summed + own_weight * spread[:, :latent]
        out = (summed / whole).astype(BF16)
        context[pl.ds(at * per_block, per_block)] = out.reshape(per_block, chunk, latent)

        def send_context(j, inner):
            peer = at * per_block + lax.rem(j + me, per_block)

            @pl.when(peer != me)
            def _():
                remote(context.at[peer], gathered.at[me], ctx_send, ctx_recv, peer).start()

            return inner

        lax.fori_loop(0, per_block, send_context, 0)
        return carry

    lax.fori_loop(0, blocks, attend, 0)
    gathered[me] = context[me]
    pltpu.make_async_copy(
        gathered.at[pl.ds(0, n - 1)], gathered.at[pl.ds(0, n - 1)], ctx_recv
    ).wait()
    pltpu.make_async_copy(
        context.at[pl.ds(0, n - 1)], context.at[pl.ds(0, n - 1)], ctx_send
    ).wait()
    everything = gathered[...].reshape(n * chunk, latent)
    for j in range(held):
        out = jnp.dot(everything, value_weight[j], preferred_element_type=F32)
        width = out.shape[1]
        out = out.reshape(n // 2, 2, held, rows, width)
        for c in range(2):
            mixed[c, :, j * width : (j + 1) * width] = (
                out[:, c, j].reshape(n // 2 * rows, width).astype(BF16)
            )


def attend(n, inverse, length, cache, queries, new_keys, value_weight):
    rows = new_keys.shape[0]
    held, latent, width = value_weight.shape
    span, depth = cache.shape[1:]
    chunk = held * rows
    vmem = pl.BlockSpec(memory_space=pltpu.VMEM)
    smem = pl.BlockSpec(memory_space=pltpu.SMEM)
    return pl.pallas_call(
        functools.partial(attend_kernel, n),
        out_shape=jax.ShapeDtypeStruct((2, n // 2 * rows, held * width), BF16),
        in_specs=[smem, smem, vmem, vmem, vmem, vmem],
        out_specs=vmem,
        scratch_shapes=[
            pltpu.VMEM((n, span, depth), BF16),
            pltpu.VMEM((n, span, depth), BF16),
            pltpu.VMEM(queries.shape, BF16),
            pltpu.VMEM((n, chunk, latent), BF16),
            pltpu.VMEM((n, chunk, latent), BF16),
            pltpu.SemaphoreType.DMA,
            pltpu.SemaphoreType.DMA,
            pltpu.SemaphoreType.DMA,
            pltpu.SemaphoreType.DMA,
        ],
        compiler_params=pltpu.CompilerParams(
            collective_id=0, has_side_effects=True, vmem_limit_bytes=40 * 2**20
        ),
        name="attend",
    )(inverse, length, cache, queries, new_keys, value_weight)


class Sum:
    def __init__(self, dims, order, where, me, bufs, recvs, send, recv):
        self.dims, self.order, self.where, self.me = dims, order, where, me
        self.strides = strides_of(dims)
        self.bufs, self.recvs, self.send, self.recv = bufs, recvs, send, recv
        self.flying = []

    def start(self, stage):
        dim = self.order[stage]
        size, at = self.dims[dim], self.where[dim]
        rest = self.bufs[stage].shape[0] // size
        for k in range(1, size):
            target = lax.rem(at + k, size)
            copy = remote(
                self.bufs[stage].at[pl.ds(target * rest, rest)],
                self.recvs[stage].at[k - 1],
                self.send.at[stage, k - 1],
                self.recv.at[stage, k - 1],
                self.me + (target - at) * self.strides[dim],
            )
            copy.start()
            self.flying.append(copy)

    def finish(self, stage):
        for copy in self.flying:
            copy.wait()
        self.flying = []
        dim = self.order[stage]
        size, at = self.dims[dim], self.where[dim]
        rest = self.bufs[stage].shape[0] // size

        def added(j):
            out = self.bufs[stage][at * rest + j].astype(F32)
            for k in range(size - 1):
                out = out + self.recvs[stage][k, j].astype(F32)
            return out

        if stage == len(self.order) - 1:
            return added(0)

        def body(j, carry):
            self.bufs[stage + 1][j] = added(j).astype(BF16)
            return carry

        lax.fori_loop(0, rest, body, 0)
        return None


def spots(dims, order, tail):
    others = dims[:-1]
    out = []
    for flat in range(tail):
        left, coords = flat, []
        for size in reversed(others):
            coords.append(left % size)
            left //= size
        coords = tuple(reversed(coords))
        spot = 0
        for dim in order[1:]:
            spot = spot * dims[dim] + coords[dim]
        out.append(spot)
    return out


def layer_kernel(dims, stages, *refs):
    n = 1
    for size in dims:
        n *= size
    orders = orders_of(dims)
    (mixed, out_weight, hidden, gain, router, picks, gate, up, down, out) = refs[:10]
    rest = list(refs[10:])

    def take(count):
        got = rest[:count]
        del rest[:count]
        return got

    wide, state, raw, act, activated = take(5)
    sums = []
    for _ in range(2):
        pair = []
        for _ in range(2):
            bufs, recvs = take(stages), take(stages)
            pair.append((bufs, recvs))
        sums.append(pair)
    parts = take(2)
    load_sem, sum_send, sum_recv, part_send, part_recv = take(5)

    me = lax.axis_index("ep")
    where = place_of(me, dims)
    strides = strides_of(dims)
    width = hidden.shape[1]
    quarter = width // 4
    tiles = quarter // TILE
    tail = n // 2
    rows = hidden.shape[0]
    core = where[-1]

    units = gate.shape[1]
    loads = [
        pltpu.make_async_copy(gate, wide.at[:, pl.ds(0, units)], load_sem.at[0]),
        pltpu.make_async_copy(up, wide.at[:, pl.ds(units, units)], load_sem.at[1]),
    ]
    for load in loads:
        load.start()

    barrier = pltpu.get_barrier_semaphore()
    peers = 0
    for dim, size in enumerate(dims):
        for k in range(1, size):
            target = lax.rem(where[dim] + k, size)
            pl.semaphore_signal(
                barrier,
                inc=1,
                device_id={"ep": me + (target - where[dim]) * strides[dim]},
                device_id_type=pl.DeviceIdType.MESH,
            )
            peers += 1
    pl.semaphore_wait(barrier, peers)

    def halves(which):
        return [
            Sum(
                dims,
                orders[h],
                where,
                me,
                *sums[which][h],
                sum_send.at[which, h],
                sum_recv.at[which, h],
            )
            for h in range(2)
        ]

    def fill(total, h, c, left, weight):
        place = spots(dims, orders[h], tail)

        def body(t, carry):
            lo = pl.multiple_of(2 * h * quarter + t * TILE, TILE)
            hi = pl.multiple_of((2 * h + 1) * quarter + t * TILE, TILE)
            rows_left = left[c]
            a = jnp.dot(rows_left, weight[:, pl.ds(lo, TILE)], preferred_element_type=F32)
            b = jnp.dot(rows_left, weight[:, pl.ds(hi, TILE)], preferred_element_type=F32)
            for i in range(tail):
                both = jnp.concatenate(
                    [a[i * rows : (i + 1) * rows], b[i * rows : (i + 1) * rows]], axis=0
                )
                total.bufs[0][
                    c * tail + place[i], :, pl.ds(pl.multiple_of(t * TILE, TILE), TILE)
                ] = both.astype(BF16)
            return carry

        lax.fori_loop(0, tiles, body, 0)

    def reduce(which, left, weight):
        total = halves(which)
        for h in range(2):
            fill(total[h], h, 1 - core, left, weight)
            total[h].start(0)
        for h in range(2):
            fill(total[h], h, core, left, weight)
        result = [None, None]
        for stage in range(stages):
            for h in range(2):
                result[h] = total[h].finish(stage)
                if stage < stages - 1:
                    total[h].start(stage + 1)
        return result

    attended = reduce(0, mixed, out_weight)

    squares = jnp.zeros((rows, 1), F32)
    for h in range(2):
        columns = [
            hidden[:, (2 * h + i) * quarter : (2 * h + i + 1) * quarter].astype(F32)
            for i in range(2)
        ]
        value = attended[h] + jnp.concatenate(columns, axis=0)
        state[h] = value
        square = jnp.sum(value * value, axis=1, keepdims=True)
        squares = squares + square[:rows] + square[rows:]
    scale = lax.rsqrt(squares / width + 1e-06)
    scale = jnp.concatenate([scale, scale], axis=0)

    mine = []
    for h in range(2):
        spot = 0
        for dim in orders[h]:
            spot = spot * dims[dim] + where[dim]
        mine.append(spot)

    experts = router.shape[0]
    logits = jnp.zeros((rows, experts), F32)
    for h in range(2):
        gains = [
            jnp.broadcast_to(gain[:, (2 * h + i) * quarter : (2 * h + i + 1) * quarter], (rows, quarter))
            for i in range(2)
        ]
        normed = (state[h] * scale * jnp.concatenate(gains, axis=0)).astype(BF16)
        parts[h][mine[h], :, pl.ds(0, quarter)] = normed
        for i in range(2):
            logits = logits + lax.dot_general(
                normed,
                router[:, (2 * h + i) * quarter : (2 * h + i + 1) * quarter],
                NT,
                preferred_element_type=F32,
            )[i * rows : (i + 1) * rows]
    lane = lax.broadcasted_iota(jnp.int32, (rows, experts), 1)
    wide_lane = lax.broadcasted_iota(jnp.int32, (rows, 128), 1)
    chosen, gates = [], []
    for k in range(picks.shape[1]):
        pick = picks[:, k : k + 1]
        logit = jnp.sum(jnp.where(lane == pick, logits, 0.0), axis=1, keepdims=True)
        gates.append(1.0 / (1.0 + jnp.exp(-logit)))
        chosen.append(pick)
    gate_sum = functools.reduce(jnp.add, gates)
    table = jnp.zeros((rows, 128), F32)
    for pick, score in zip(chosen, gates):
        table = table + jnp.where(wide_lane == pick, ROUTE_SCALE * score / gate_sum, 0.0)
    high = table.astype(BF16).astype(F32)
    parts[0][mine[0], :, pl.ds(quarter, 128)] = jnp.concatenate(
        [high, table - high], axis=0
    ).astype(BF16)

    starts, counts = list(mine), [1, 1]
    for stage in reversed(range(stages)):
        flying = []
        for h in range(2):
            dim = orders[h][stage]
            size, at = dims[dim], where[dim]
            block = parts[h].at[pl.ds(starts[h], counts[h])]
            for k in range(1, size):
                target = lax.rem(at + k, size)
                copy = remote(
                    block,
                    block,
                    part_send.at[h, stage, k - 1],
                    part_recv.at[h, stage, k - 1],
                    me + (target - at) * strides[dim],
                )
                copy.start()
                flying.append(copy)
            starts[h] = starts[h] - at * counts[h]
            counts[h] = counts[h] * size
        for copy in flying:
            copy.wait()
    for load in loads:
        load.wait()

    expert = lax.div(me, SPLIT)
    for h in range(2):
        place = spots(dims, orders[h], tail)
        for c in range(2):
            rows_in = parts[h][c * tail : (c + 1) * tail, :, :quarter].reshape(tail * 2 * rows, quarter)
            for i in range(2):
                begin = (2 * h + i) * quarter
                product = jnp.dot(
                    rows_in, wide[begin : begin + quarter, :], preferred_element_type=F32
                ).reshape(tail, 2 * rows, 2 * units)
                raw[i] = product
            for j in range(tail):
                block = raw[0, place[j], :rows] + raw[1, place[j], rows:]
                if h == 0:
                    act[c, j] = block
                else:
                    act[c, j] = act[c, j] + block
    lane = lax.broadcasted_iota(jnp.int32, (rows, 128), 1)
    place = spots(dims, orders[0], tail)

    def activate(c):
        out_rows = []
        for j in range(tail):
            both = act[c, j]
            g, u = both[:, :units], both[:, units:]
            table = parts[0][c * tail + place[j], :, pl.ds(quarter, 128)].astype(F32)
            share = jnp.where(lane == expert, table[:rows] + table[rows:], 0.0)
            share = jnp.sum(share, axis=1, keepdims=True)
            out_rows.append(g / (1.0 + jnp.exp(-g)) * u * share)
        return jnp.concatenate(out_rows, axis=0).astype(BF16)

    for c in range(2):
        activated[c] = activate(c)
    combined = reduce(1, activated, down)
    for h in range(2):
        value = state[h] + combined[h]
        for i in range(2):
            out[:, (2 * h + i) * quarter : (2 * h + i + 1) * quarter] = value[
                i * rows : (i + 1) * rows
            ].astype(BF16)


def layer(dims, mixed, out_weight, hidden, gain, router, picks, gate, up, down):
    orders = orders_of(dims)
    stages = len(dims)
    n = mixed.shape[0] * mixed.shape[1] // hidden.shape[0]
    rows, width = hidden.shape
    quarter, tail, units = width // 4, n // 2, gate.shape[1]
    most = max(dims) - 1
    vmem = pl.BlockSpec(memory_space=pltpu.VMEM)
    anywhere = pl.BlockSpec(memory_space=pl.ANY)
    scratch = [
        pltpu.VMEM((width, 2 * units), BF16),
        pltpu.VMEM((2, 2 * rows, quarter), F32),
        pltpu.VMEM((2, tail, 2 * rows, 2 * units), F32),
        pltpu.VMEM((2, tail, rows, 2 * units), F32),
        pltpu.VMEM((2, tail * rows, units), BF16),
    ]
    for _ in range(2):
        for h in range(2):
            bufs, recvs, left = [], [], n
            for dim in orders[h]:
                size = dims[dim]
                bufs.append(pltpu.VMEM((left, 2 * rows, quarter), BF16))
                left //= size
                recvs.append(pltpu.VMEM((size - 1, left, 2 * rows, quarter), BF16))
            scratch += bufs + recvs
    scratch += [
        pltpu.VMEM((n, 2 * rows, quarter + 128), BF16),
        pltpu.VMEM((n, 2 * rows, quarter), BF16),
        pltpu.SemaphoreType.DMA((2,)),
        pltpu.SemaphoreType.DMA((2, 2, stages, most)),
        pltpu.SemaphoreType.DMA((2, 2, stages, most)),
        pltpu.SemaphoreType.DMA((2, stages, most)),
        pltpu.SemaphoreType.DMA((2, stages, most)),
    ]
    return pl.pallas_call(
        functools.partial(layer_kernel, dims, stages),
        out_shape=jax.ShapeDtypeStruct(hidden.shape, BF16),
        in_specs=[vmem, vmem, vmem, vmem, vmem, vmem, anywhere, anywhere, vmem],
        out_specs=vmem,
        scratch_shapes=scratch,
        compiler_params=pltpu.CompilerParams(
            collective_id=1, has_side_effects=True, vmem_limit_bytes=60 * 2**20
        ),
        name="layer",
    )(mixed, out_weight, hidden, gain, router, picks, gate, up, down)


def shards(
    dims,
    cache_src,
    lengths,
    placement,
    queries,
    new_keys,
    hidden,
    latent_value_weight,
    out_weight,
    norm_gain,
    router,
    expert_picks,
    gate_weight,
    up_weight,
    down_weight,
):
    n = lax.axis_size("ep")
    me = lax.axis_index("ep")
    request_ids = jnp.arange(n, dtype=jnp.int32)
    inverse = jnp.sum(
        jnp.where(placement[None, :] == request_ids[:, None], request_ids[None, :], 0), axis=1
    ).astype(jnp.int32)
    length = jnp.sum(jnp.where(placement == me, lengths, 0)).astype(jnp.int32).reshape(1)
    mixed = attend(
        n,
        inverse,
        length,
        cache_src.reshape(cache_src.shape[2:]),
        queries.reshape(-1, queries.shape[2]),
        new_keys,
        latent_value_weight,
    )
    return layer(
        dims,
        mixed,
        out_weight,
        hidden,
        norm_gain.reshape(1, -1),
        router,
        expert_picks,
        gate_weight,
        up_weight,
        down_weight,
    )


def solution(mesh):
    in_specs = (
        P(("groups", "ep"), None, None, None, None),
        P("groups"),
        P("groups"),
        P(("groups", "ep"), None, None),
        P(("groups", "ep"), None),
        P(("groups", "ep"), None),
        P("ep", None, None),
        P("ep", None),
        P(),
        P(),
        P(("groups", "ep"), None),
        P(None, "ep"),
        P(None, "ep"),
        P("ep", None),
    )
    out_specs = P(("groups", "ep"), None)
    return jax.shard_map(
        functools.partial(shards, dims_of(mesh)),
        mesh=mesh,
        in_specs=in_specs,
        out_specs=out_specs,
        check_vma=False,
    )
```

```python
import functools

import jax
import jax.numpy as jnp
from jax import lax
from jax.experimental import pallas as pl
from jax.experimental.pallas import tpu as pltpu
from jax.sharding import PartitionSpec as P

SPLIT = 8
SCORE_SCALE = 192.0 ** (-0.5)
ROUTE_SCALE = 2.5
PARTS = 3
F32 = jnp.float32
BF16 = jnp.bfloat16
NT = (((1,), (1,)), ((), ()))


def dims_of(mesh):
    n = mesh.shape["ep"]
    if mesh.shape["groups"] == 1 and n % 16 == 0:
        return (n // 16, 2, 2, 2, 2)
    return (n // 2, 2)


def orders_of(dims):
    if len(dims) == 5:
        return ((4, 3, 2, 1, 0), (4, 2, 1, 3, 0), (4, 1, 3, 2, 0))
    return ((1, 0),) * 3


def cuts_of(width):
    lanes = width // 256
    sizes = [lanes // 3 + (1 if p < lanes % 3 else 0) for p in range(3)]
    out, begin = [], 0
    for size in sizes:
        out.append((begin, size * 128))
        begin += size * 256
    return tuple(out)


def tile_of(run):
    for tile in (384, 256, 128):
        if run % tile == 0:
            return tile
    return run


def strides_of(dims):
    out, step = [], 1
    for size in reversed(dims):
        out.append(step)
        step *= size
    return tuple(reversed(out))


def place_of(flat, dims):
    out = []
    for size in reversed(dims):
        out.append(lax.rem(flat, size))
        flat = lax.div(flat, size)
    return tuple(reversed(out))


def remote(src, dst, send, recv, target):
    return pltpu.make_async_remote_copy(
        src_ref=src,
        dst_ref=dst,
        send_sem=send,
        recv_sem=recv,
        device_id={"ep": target},
        device_id_type=pl.DeviceIdType.MESH,
    )


def attend_kernel(
    n,
    facts,
    cache,
    queries_in,
    new_keys,
    value_weight_in,
    mixed,
    queries,
    value_weight,
    staged,
    keys,
    by_head,
    context,
    gathered,
    load_sem,
    key_send,
    key_recv,
    ctx_send,
    ctx_recv,
):
    me = lax.axis_index("ep")
    rows, latent = new_keys.shape[0], value_weight.shape[1]
    total_rows = queries.shape[0]
    heads = total_rows // rows
    held = value_weight.shape[0]
    chunk = held * rows
    span = keys.shape[1]
    loads = [
        pltpu.make_async_copy(queries_in, queries, load_sem.at[0]),
        pltpu.make_async_copy(value_weight_in, value_weight, load_sem.at[1]),
    ]
    for load in loads:
        load.start()
    barrier = pltpu.get_barrier_semaphore()

    def greet(k, carry):
        pl.semaphore_signal(
            barrier,
            inc=1,
            device_id={"ep": lax.rem(me + k, n)},
            device_id_type=pl.DeviceIdType.MESH,
        )
        return carry

    lax.fori_loop(1, n, greet, 0)
    pl.semaphore_wait(barrier, n - 1)

    def send_keys(k, carry):
        peer = lax.rem(me + k, n)
        staged[peer] = cache[facts[peer]]
        remote(staged.at[peer], keys.at[me], key_send, key_recv, peer).start()
        return carry

    lax.fori_loop(1, n, send_keys, 0)
    keys[me] = cache[facts[me]]

    to = lax.broadcasted_iota(jnp.int32, (total_rows, total_rows), 0)
    source = lax.broadcasted_iota(jnp.int32, (total_rows, total_rows), 1)
    moved = (lax.rem(to, rows) * heads + lax.div(to, rows) == source).astype(BF16)
    loads[0].wait()
    by_head[...] = jnp.dot(moved, queries[...], preferred_element_type=F32).astype(BF16)

    wait_rest = pltpu.make_async_copy(keys.at[pl.ds(0, n - 1)], keys.at[pl.ds(0, n - 1)], key_recv)
    wait_rest.wait()
    pltpu.make_async_copy(staged.at[pl.ds(0, n - 1)], staged.at[pl.ds(0, n - 1)], key_send).wait()

    block = min(total_rows, 128)
    blocks = total_rows // block
    per_block = block // chunk
    live = facts[n]
    first = lax.div(me, per_block)

    def attend(step, carry):
        at = lax.rem(first + 1 + step, blocks)
        begin = pl.multiple_of(at * block, block)
        q = by_head[pl.ds(begin, block), :]
        key_rows = keys[...].reshape(n * span, keys.shape[2])
        own_keys = new_keys[...].astype(F32)
        spread = jnp.broadcast_to(own_keys[None], (block // rows,) + own_keys.shape)
        spread = spread.reshape(block, own_keys.shape[1])
        own = jnp.sum(q.astype(F32) * spread, axis=1, keepdims=True) * SCORE_SCALE
        scores = lax.dot_general(q, key_rows, NT, preferred_element_type=F32) * SCORE_SCALE
        position = lax.broadcasted_iota(jnp.int32, scores.shape, 1)
        scores = jnp.where(position < live, scores, -jnp.inf)
        top = jnp.maximum(jnp.max(scores, axis=1, keepdims=True), own)
        weights = jnp.exp(scores - top).astype(BF16)
        own_weight = jnp.exp(own - top).astype(BF16).astype(F32)
        whole = jnp.sum(weights.astype(F32), axis=1, keepdims=True) + own_weight
        summed = jnp.dot(weights, key_rows[:, :latent], preferred_element_type=F32)
        summed = summed + own_weight * spread[:, :latent]
        out = (summed / whole).astype(BF16)
        context[pl.ds(at * per_block, per_block)] = out.reshape(per_block, chunk, latent)

        def send_context(j, inner):
            peer = at * per_block + lax.rem(j + me, per_block)

            @pl.when(peer != me)
            def _():
                remote(context.at[peer], gathered.at[me], ctx_send, ctx_recv, peer).start()

            return inner

        lax.fori_loop(0, per_block, send_context, 0)
        return carry

    lax.fori_loop(0, blocks, attend, 0)
    gathered[me] = context[me]
    pltpu.make_async_copy(
        gathered.at[pl.ds(0, n - 1)], gathered.at[pl.ds(0, n - 1)], ctx_recv
    ).wait()
    pltpu.make_async_copy(
        context.at[pl.ds(0, n - 1)], context.at[pl.ds(0, n - 1)], ctx_send
    ).wait()
    loads[1].wait()
    everything = gathered[...].reshape(n * chunk, latent)
    for j in range(held):
        out = jnp.dot(everything, value_weight[j], preferred_element_type=F32)
        width = out.shape[1]
        out = out.reshape(n // 2, 2, held, rows, width)
        for c in range(2):
            mixed[c, :, j * width : (j + 1) * width] = (
                out[:, c, j].reshape(n // 2 * rows, width).astype(BF16)
            )


def attend(n, facts, cache, queries, new_keys, value_weight):
    rows = new_keys.shape[0]
    held, latent, width = value_weight.shape
    span, depth = cache.shape[1:]
    chunk = held * rows
    vmem = pl.BlockSpec(memory_space=pltpu.VMEM)
    smem = pl.BlockSpec(memory_space=pltpu.SMEM)
    anywhere = pl.BlockSpec(memory_space=pl.ANY)
    return pl.pallas_call(
        functools.partial(attend_kernel, n),
        out_shape=jax.ShapeDtypeStruct((2, n // 2 * rows, held * width), BF16),
        in_specs=[smem, vmem, anywhere, vmem, anywhere],
        out_specs=vmem,
        scratch_shapes=[
            pltpu.VMEM(queries.shape, BF16),
            pltpu.VMEM(value_weight.shape, BF16),
            pltpu.VMEM((n, span, depth), BF16),
            pltpu.VMEM((n, span, depth), BF16),
            pltpu.VMEM(queries.shape, BF16),
            pltpu.VMEM((n, chunk, latent), BF16),
            pltpu.VMEM((n, chunk, latent), BF16),
            pltpu.SemaphoreType.DMA((2,)),
            pltpu.SemaphoreType.DMA,
            pltpu.SemaphoreType.DMA,
            pltpu.SemaphoreType.DMA,
            pltpu.SemaphoreType.DMA,
        ],
        compiler_params=pltpu.CompilerParams(
            collective_id=0, has_side_effects=True, vmem_limit_bytes=40 * 2**20
        ),
        name="attend",
    )(facts, cache, queries, new_keys, value_weight)


class Sum:
    def __init__(self, dims, order, where, me, bufs, recvs, send, recv):
        self.dims, self.order, self.where, self.me = dims, order, where, me
        self.strides = strides_of(dims)
        self.bufs, self.recvs, self.send, self.recv = bufs, recvs, send, recv
        self.flying = []

    def start(self, stage):
        dim = self.order[stage]
        size, at = self.dims[dim], self.where[dim]
        rest = self.bufs[stage].shape[0] // size
        for k in range(1, size):
            target = lax.rem(at + k, size)
            copy = remote(
                self.bufs[stage].at[pl.ds(target * rest, rest)],
                self.recvs[stage].at[k - 1],
                self.send.at[stage, k - 1],
                self.recv.at[stage, k - 1],
                self.me + (target - at) * self.strides[dim],
            )
            copy.start()
            self.flying.append(copy)

    def finish(self, stage):
        for copy in self.flying:
            copy.wait()
        self.flying = []
        dim = self.order[stage]
        size, at = self.dims[dim], self.where[dim]
        rest = self.bufs[stage].shape[0] // size

        def added(j):
            out = self.bufs[stage][at * rest + j].astype(F32)
            for k in range(size - 1):
                out = out + self.recvs[stage][k, j].astype(F32)
            return out

        if stage == len(self.order) - 1:
            return added(0)

        def body(j, carry):
            self.bufs[stage + 1][j] = added(j).astype(BF16)
            return carry

        lax.fori_loop(0, rest, body, 0)
        return None


def spots(dims, order, tail):
    others = dims[:-1]
    out = []
    for flat in range(tail):
        left, coords = flat, []
        for size in reversed(others):
            coords.append(left % size)
            left //= size
        coords = tuple(reversed(coords))
        spot = 0
        for dim in order[1:]:
            spot = spot * dims[dim] + coords[dim]
        out.append(spot)
    return out


def layer_kernel(dims, stages, *refs):
    n = 1
    for size in dims:
        n *= size
    orders = orders_of(dims)
    (mixed, out_weight, hidden, gain, router, picks, gate, up, down, out) = refs[:10]
    rest = list(refs[10:])

    def take(count):
        got = rest[:count]
        del rest[:count]
        return got

    wide, raw, act, activated = take(4)
    state = take(PARTS)
    sums = []
    for _ in range(2):
        sums.append([(take(stages), take(stages)) for _ in range(PARTS)])
    parts = take(PARTS)
    load_sem, sum_send, sum_recv, part_send, part_recv, pass_send, pass_recv = take(7)

    me = lax.axis_index("ep")
    where = place_of(me, dims)
    strides = strides_of(dims)
    width = hidden.shape[1]
    cuts = cuts_of(width)
    tail = n // 2
    rows = hidden.shape[0]
    core = where[-1]

    def runs(p):
        begin, run = cuts[p]
        return [(begin, begin + run), (begin + run, begin + 2 * run)]

    units = gate.shape[1]
    loads = [
        pltpu.make_async_copy(gate, wide.at[:, pl.ds(0, units)], load_sem.at[0]),
        pltpu.make_async_copy(up, wide.at[:, pl.ds(units, units)], load_sem.at[1]),
    ]
    for load in loads:
        load.start()

    barrier = pltpu.get_barrier_semaphore()
    peers = 0
    for dim, size in enumerate(dims):
        for k in range(1, size):
            target = lax.rem(where[dim] + k, size)
            pl.semaphore_signal(
                barrier,
                inc=1,
                device_id={"ep": me + (target - where[dim]) * strides[dim]},
                device_id_type=pl.DeviceIdType.MESH,
            )
            peers += 1
    pl.semaphore_wait(barrier, peers)

    def fill(total, p, c, left, weight):
        place = spots(dims, orders[p], tail)
        begin, run = cuts[p]
        tile = tile_of(run)

        def body(t, carry):
            lo = pl.multiple_of(begin + t * tile, 128)
            hi = pl.multiple_of(begin + run + t * tile, 128)
            at = pl.multiple_of(t * tile, 128)
            rows_left = left[c]
            a = jnp.dot(rows_left, weight[:, pl.ds(lo, tile)], preferred_element_type=F32)
            b = jnp.dot(rows_left, weight[:, pl.ds(hi, tile)], preferred_element_type=F32)
            for i in range(tail):
                both = jnp.concatenate(
                    [a[i * rows : (i + 1) * rows], b[i * rows : (i + 1) * rows]], axis=0
                )
                total.bufs[0][c * tail + place[i], :, pl.ds(at, tile)] = both.astype(BF16)
            return carry

        lax.fori_loop(0, run // tile, body, 0)

    def reduce(which, left, weight):
        total = [
            Sum(
                dims,
                orders[p],
                where,
                me,
                *sums[which][p],
                sum_send.at[which, p],
                sum_recv.at[which, p],
            )
            for p in range(PARTS)
        ]
        for p in range(PARTS):
            fill(total[p], p, 1 - core, left, weight)
            total[p].start(0)
        result = [None] * PARTS
        for stage in range(stages):
            for p in range(PARTS):
                if stage == 0:
                    fill(total[p], p, core, left, weight)
                result[p] = total[p].finish(stage)
                if stage < stages - 1:
                    total[p].start(stage + 1)
        return result

    attended = reduce(0, mixed, out_weight)

    squares = jnp.zeros((rows, 1), F32)
    for p in range(PARTS):
        columns = [hidden[:, lo:hi].astype(F32) for lo, hi in runs(p)]
        value = attended[p] + jnp.concatenate(columns, axis=0)
        state[p][...] = value
        square = jnp.sum(value * value, axis=1, keepdims=True)
        squares = squares + square[:rows] + square[rows:]
    scale = lax.rsqrt(squares / width + 1e-06)
    scale = jnp.concatenate([scale, scale], axis=0)

    mine = []
    for p in range(PARTS):
        spot = 0
        for dim in orders[p]:
            spot = spot * dims[dim] + where[dim]
        mine.append(spot)

    flying = [[] for _ in range(PARTS)]
    passed = [[] for _ in range(PARTS)]
    starts, counts = list(mine), [1] * PARTS

    def send_part(p, stage):
        dim = orders[p][stage]
        size, at = dims[dim], where[dim]
        block = parts[p].at[pl.ds(starts[p], counts[p])]
        for k in range(1, size):
            target = lax.rem(at + k, size)
            copy = remote(
                block,
                block,
                part_send.at[p, stage, k - 1],
                part_recv.at[p, stage, k - 1],
                me + (target - at) * strides[dim],
            )
            copy.start()
            flying[p].append(copy)

    def pass_on(p, begin, count, stage, k):
        block = parts[p].at[pl.ds(begin, count)]
        copy = remote(
            block, block, pass_send.at[p, stage, k], pass_recv.at[p, stage, k], me + 1 - 2 * core
        )
        copy.start()
        passed[p].append(copy)

    def take_part(p, stage):
        for copy in flying[p]:
            copy.wait()
        flying[p].clear()
        dim = orders[p][stage]
        size, at = dims[dim], where[dim]
        base = starts[p] - at * counts[p]
        fresh = [(base + lax.rem(at + k, size) * counts[p], counts[p]) for k in range(1, size)]
        starts[p] = base
        counts[p] = counts[p] * size
        return fresh

    experts = router.shape[0]
    logits = jnp.zeros((rows, experts), F32)
    for p in reversed(range(PARTS)):
        run = cuts[p][1]
        gains = [jnp.broadcast_to(gain[:, lo:hi], (rows, run)) for lo, hi in runs(p)]
        normed = (state[p][...] * scale * jnp.concatenate(gains, axis=0)).astype(BF16)
        parts[p][mine[p], :, pl.ds(0, run)] = normed
        if p > 0:
            send_part(p, stages - 1)
        for i, (lo, hi) in enumerate(runs(p)):
            logits = logits + lax.dot_general(
                normed, router[:, lo:hi], NT, preferred_element_type=F32
            )[i * rows : (i + 1) * rows]
    lane = lax.broadcasted_iota(jnp.int32, (rows, experts), 1)
    wide_lane = lax.broadcasted_iota(jnp.int32, (rows, 128), 1)
    chosen, gates = [], []
    for k in range(picks.shape[1]):
        pick = picks[:, k : k + 1]
        logit = jnp.sum(jnp.where(lane == pick, logits, 0.0), axis=1, keepdims=True)
        gates.append(1.0 / (1.0 + jnp.exp(-logit)))
        chosen.append(pick)
    gate_sum = functools.reduce(jnp.add, gates)
    table = jnp.zeros((rows, 128), F32)
    for pick, score in zip(chosen, gates):
        table = table + jnp.where(wide_lane == pick, ROUTE_SCALE * score / gate_sum, 0.0)
    high = table.astype(BF16).astype(F32)
    share_at = cuts[0][1]
    parts[0][mine[0], :, pl.ds(share_at, 128)] = jnp.concatenate(
        [high, table - high], axis=0
    ).astype(BF16)
    send_part(0, stages - 1)

    turns = list(range(1, PARTS)) + [0]
    for p in turns:
        pass_on(p, mine[p], 1, 0, 0)
    for stage in reversed(range(1, stages)):
        for p in turns:
            fresh = take_part(p, stage)
            if stage > 1:
                send_part(p, stage - 1)
            for k, (begin, count) in enumerate(fresh):
                pass_on(p, begin, count, stage, k)
    for load in loads:
        load.wait()

    def expand(p, c):
        place = spots(dims, orders[p], tail)
        run = cuts[p][1]
        rows_in = parts[p][pl.ds(c * tail, tail), :, pl.ds(0, run)]
        rows_in = rows_in.reshape(tail * 2 * rows, run)
        for i, (lo, hi) in enumerate(runs(p)):
            raw[i] = jnp.dot(rows_in, wide[lo:hi, :], preferred_element_type=F32).reshape(
                tail, 2 * rows, 2 * units
            )
        for j in range(tail):
            block = raw[0, place[j], :rows] + raw[1, place[j], rows:]
            if p == turns[0]:
                act[j] = block
            else:
                act[j] = act[j] + block

    expert = lax.div(me, SPLIT)
    lane = lax.broadcasted_iota(jnp.int32, (rows, 128), 1)
    place = spots(dims, orders[0], tail)

    def activate(c):
        out_rows = []
        for j in range(tail):
            both = act[j]
            g, u = both[:, :units], both[:, units:]
            table = parts[0][c * tail + place[j], :, pl.ds(share_at, 128)].astype(F32)
            share = jnp.where(lane == expert, table[:rows] + table[rows:], 0.0)
            share = jnp.sum(share, axis=1, keepdims=True)
            out_rows.append(g / (1.0 + jnp.exp(-g)) * u * share)
        activated[c] = jnp.concatenate(out_rows, axis=0).astype(BF16)

    for p in turns:
        expand(p, core)
    activate(core)
    for p in turns:
        for copy in passed[p]:
            copy.wait()
        expand(p, 1 - core)
    activate(1 - core)
    combined = reduce(1, activated, down)
    for p in range(PARTS):
        value = state[p][...] + combined[p]
        for i, (lo, hi) in enumerate(runs(p)):
            out[:, lo:hi] = value[i * rows : (i + 1) * rows].astype(BF16)


def layer(dims, mixed, out_weight, hidden, gain, router, picks, gate, up, down):
    orders = orders_of(dims)
    stages = len(dims)
    n = mixed.shape[0] * mixed.shape[1] // hidden.shape[0]
    rows, width = hidden.shape
    cuts = cuts_of(width)
    tail, units = n // 2, gate.shape[1]
    most = max(dims) - 1
    vmem = pl.BlockSpec(memory_space=pltpu.VMEM)
    anywhere = pl.BlockSpec(memory_space=pl.ANY)
    scratch = [
        pltpu.VMEM((width, 2 * units), BF16),
        pltpu.VMEM((2, tail, 2 * rows, 2 * units), F32),
        pltpu.VMEM((tail, rows, 2 * units), F32),
        pltpu.VMEM((2, tail * rows, units), BF16),
    ]
    scratch += [pltpu.VMEM((2 * rows, run), F32) for _, run in cuts]
    for _ in range(2):
        for p in range(PARTS):
            run = cuts[p][1]
            bufs, recvs, left = [], [], n
            for dim in orders[p]:
                size = dims[dim]
                bufs.append(pltpu.VMEM((left, 2 * rows, run), BF16))
                left //= size
                recvs.append(pltpu.VMEM((size - 1, left, 2 * rows, run), BF16))
            scratch += bufs + recvs
    scratch += [
        pltpu.VMEM((n, 2 * rows, cuts[p][1] + (128 if p == 0 else 0)), BF16) for p in range(PARTS)
    ]
    scratch += [
        pltpu.SemaphoreType.DMA((2,)),
        pltpu.SemaphoreType.DMA((2, PARTS, stages, most)),
        pltpu.SemaphoreType.DMA((2, PARTS, stages, most)),
        pltpu.SemaphoreType.DMA((PARTS, stages, most)),
        pltpu.SemaphoreType.DMA((PARTS, stages, most)),
        pltpu.SemaphoreType.DMA((PARTS, stages, most)),
        pltpu.SemaphoreType.DMA((PARTS, stages, most)),
    ]
    return pl.pallas_call(
        functools.partial(layer_kernel, dims, stages),
        out_shape=jax.ShapeDtypeStruct(hidden.shape, BF16),
        in_specs=[vmem, vmem, vmem, vmem, vmem, vmem, anywhere, anywhere, vmem],
        out_specs=vmem,
        scratch_shapes=scratch,
        compiler_params=pltpu.CompilerParams(
            collective_id=1, has_side_effects=True, vmem_limit_bytes=60 * 2**20
        ),
        name="layer",
    )(mixed, out_weight, hidden, gain, router, picks, gate, up, down)


def shards(
    dims,
    cache_src,
    lengths,
    placement,
    queries,
    new_keys,
    hidden,
    latent_value_weight,
    out_weight,
    norm_gain,
    router,
    expert_picks,
    gate_weight,
    up_weight,
    down_weight,
):
    n = lax.axis_size("ep")
    me = lax.axis_index("ep")
    request_ids = jnp.arange(n, dtype=jnp.int32)[None, :]
    slots = jnp.arange(n + 1, dtype=jnp.int32)[:, None]
    named = jnp.where(slots < n, request_ids, lengths[None, :])
    facts = jnp.sum(
        jnp.where(placement[None, :] == jnp.where(slots < n, slots, me), named, 0), axis=1
    ).astype(jnp.int32)
    mixed = attend(
        n,
        facts,
        cache_src.reshape(cache_src.shape[2:]),
        queries.reshape(-1, queries.shape[2]),
        new_keys,
        latent_value_weight,
    )
    return layer(
        dims,
        mixed,
        out_weight,
        hidden,
        norm_gain.reshape(1, -1),
        router,
        expert_picks,
        gate_weight,
        up_weight,
        down_weight,
    )


def solution(mesh):
    in_specs = (
        P(("groups", "ep"), None, None, None, None),
        P("groups"),
        P("groups"),
        P(("groups", "ep"), None, None),
        P(("groups", "ep"), None),
        P(("groups", "ep"), None),
        P("ep", None, None),
        P("ep", None),
        P(),
        P(),
        P(("groups", "ep"), None),
        P(None, "ep"),
        P(None, "ep"),
        P("ep", None),
    )
    out_specs = P(("groups", "ep"), None)
    return jax.shard_map(
        functools.partial(shards, dims_of(mesh)),
        mesh=mesh,
        in_specs=in_specs,
        out_specs=out_specs,
        check_vma=False,
    )
```

```python
import functools
import math

import jax
import jax.numpy as jnp
from jax import lax
from jax.experimental import pallas as pl
from jax.experimental.pallas import tpu as pltpu
from jax.sharding import PartitionSpec as P

SPLIT = 8
SCORE_SCALE = 192.0 ** (-0.5)
ROUTE_SCALE = 2.5
PARTS = 3
F32 = jnp.float32
BF16 = jnp.bfloat16
NT = (((1,), (1,)), ((), ()))


def dims_of(mesh):
    n = mesh.shape["ep"]
    if mesh.shape["groups"] == 1 and n % 16 == 0:
        return (n // 16, 2, 2, 2, 2)
    return (n // 2, 2)


def orders_of(dims):
    if len(dims) == 5:
        return ((4, 3, 2, 1, 0), (4, 2, 1, 3, 0), (4, 1, 3, 2, 0))
    return ((1, 0),) * 3


def cuts_of(width):
    lanes = width // 256
    sizes = [lanes // 3 + (1 if p < lanes % 3 else 0) for p in range(3)]
    out, begin = [], 0
    for size in sizes:
        out.append((begin, size * 128))
        begin += size * 256
    return tuple(out)


def tile_of(run):
    for tile in (384, 256, 128):
        if run % tile == 0:
            return tile
    return run


def strides_of(dims):
    out, step = [], 1
    for size in reversed(dims):
        out.append(step)
        step *= size
    return tuple(reversed(out))


def place_of(flat, dims):
    out = []
    for size in reversed(dims):
        out.append(lax.rem(flat, size))
        flat = lax.div(flat, size)
    return tuple(reversed(out))


def remote(src, dst, send, recv, target):
    return pltpu.make_async_remote_copy(
        src_ref=src,
        dst_ref=dst,
        send_sem=send,
        recv_sem=recv,
        device_id={"ep": target},
        device_id_type=pl.DeviceIdType.MESH,
    )


def attend_kernel(
    n,
    facts,
    cache_in,
    queries_in,
    new_keys,
    value_weight_in,
    mixed,
    cache,
    queries,
    value_weight,
    staged,
    keys,
    by_head,
    context,
    gathered,
    load_sem,
    key_send,
    key_recv,
    ctx_send,
    ctx_recv,
):
    me = lax.axis_index("ep")
    rows, latent = new_keys.shape[0], value_weight.shape[1]
    mix = next(m for m in (11, 13, 17, 19, 1) if math.gcd(m, n) == 1)
    total_rows = queries.shape[0]
    heads = total_rows // rows
    held = value_weight.shape[0]
    chunk = held * rows
    span = keys.shape[1]
    loads = [
        pltpu.make_async_copy(queries_in, queries, load_sem.at[0]),
        pltpu.make_async_copy(value_weight_in, value_weight, load_sem.at[1]),
        pltpu.make_async_copy(cache_in, cache, load_sem.at[2]),
    ]
    for load in (loads[2], loads[0], loads[1]):
        load.start()
    barrier = pltpu.get_barrier_semaphore()

    def greet(k, carry):
        pl.semaphore_signal(
            barrier,
            inc=1,
            device_id={"ep": lax.rem(me + k, n)},
            device_id_type=pl.DeviceIdType.MESH,
        )
        return carry

    lax.fori_loop(1, n, greet, 0)
    pl.semaphore_wait(barrier, n - 1)

    loads[2].wait()

    def send_keys(k, carry):
        peer = lax.rem(me + lax.rem(k * mix, n), n)
        staged[peer] = cache[facts[peer]]
        remote(staged.at[peer], keys.at[me], key_send, key_recv, peer).start()
        return carry

    lax.fori_loop(1, n, send_keys, 0)
    keys[me] = cache[facts[me]]

    to = lax.broadcasted_iota(jnp.int32, (total_rows, total_rows), 0)
    source = lax.broadcasted_iota(jnp.int32, (total_rows, total_rows), 1)
    moved = (lax.rem(to, rows) * heads + lax.div(to, rows) == source).astype(BF16)
    loads[0].wait()
    by_head[...] = jnp.dot(moved, queries[...], preferred_element_type=F32).astype(BF16)

    wait_rest = pltpu.make_async_copy(keys.at[pl.ds(0, n - 1)], keys.at[pl.ds(0, n - 1)], key_recv)
    wait_rest.wait()
    pltpu.make_async_copy(staged.at[pl.ds(0, n - 1)], staged.at[pl.ds(0, n - 1)], key_send).wait()

    block = min(total_rows, 128)
    blocks = total_rows // block
    per_block = block // chunk
    live = facts[n]
    first = lax.div(me, per_block)

    def attend(step, carry):
        at = lax.rem(first + 1 + step, blocks)
        begin = pl.multiple_of(at * block, block)
        q = by_head[pl.ds(begin, block), :]
        key_rows = keys[...].reshape(n * span, keys.shape[2])
        own_keys = new_keys[...].astype(F32)
        spread = jnp.broadcast_to(own_keys[None], (block // rows,) + own_keys.shape)
        spread = spread.reshape(block, own_keys.shape[1])
        own = jnp.sum(q.astype(F32) * spread, axis=1, keepdims=True) * SCORE_SCALE
        scores = lax.dot_general(q, key_rows, NT, preferred_element_type=F32) * SCORE_SCALE
        position = lax.broadcasted_iota(jnp.int32, scores.shape, 1)
        scores = jnp.where(position < live, scores, -jnp.inf)
        top = jnp.maximum(jnp.max(scores, axis=1, keepdims=True), own)
        weights = jnp.exp(scores - top).astype(BF16)
        own_weight = jnp.exp(own - top).astype(BF16).astype(F32)
        whole = jnp.sum(weights.astype(F32), axis=1, keepdims=True) + own_weight
        summed = jnp.dot(weights, key_rows[:, :latent], preferred_element_type=F32)
        summed = summed + own_weight * spread[:, :latent]
        out = (summed / whole).astype(BF16)
        context[pl.ds(at * per_block, per_block)] = out.reshape(per_block, chunk, latent)

        def send_context(j, inner):
            peer = at * per_block + lax.rem(j + me, per_block)

            @pl.when(peer != me)
            def _():
                remote(context.at[peer], gathered.at[me], ctx_send, ctx_recv, peer).start()

            return inner

        lax.fori_loop(0, per_block, send_context, 0)
        return carry

    lax.fori_loop(0, blocks, attend, 0)
    gathered[me] = context[me]
    pltpu.make_async_copy(
        gathered.at[pl.ds(0, n - 1)], gathered.at[pl.ds(0, n - 1)], ctx_recv
    ).wait()
    pltpu.make_async_copy(
        context.at[pl.ds(0, n - 1)], context.at[pl.ds(0, n - 1)], ctx_send
    ).wait()
    loads[1].wait()
    everything = gathered[...].reshape(n * chunk, latent)
    for j in range(held):
        out = jnp.dot(everything, value_weight[j], preferred_element_type=F32)
        width = out.shape[1]
        out = out.reshape(n // 2, 2, held, rows, width)
        for c in range(2):
            mixed[c, :, j * width : (j + 1) * width] = (
                out[:, c, j].reshape(n // 2 * rows, width).astype(BF16)
            )


def attend(n, facts, cache, queries, new_keys, value_weight):
    rows = new_keys.shape[0]
    held, latent, width = value_weight.shape
    span, depth = cache.shape[1:]
    chunk = held * rows
    vmem = pl.BlockSpec(memory_space=pltpu.VMEM)
    smem = pl.BlockSpec(memory_space=pltpu.SMEM)
    anywhere = pl.BlockSpec(memory_space=pl.ANY)
    return pl.pallas_call(
        functools.partial(attend_kernel, n),
        out_shape=jax.ShapeDtypeStruct((2, n // 2 * rows, held * width), BF16),
        in_specs=[smem, anywhere, anywhere, vmem, anywhere],
        out_specs=vmem,
        scratch_shapes=[
            pltpu.VMEM(cache.shape, BF16),
            pltpu.VMEM(queries.shape, BF16),
            pltpu.VMEM(value_weight.shape, BF16),
            pltpu.VMEM((n, span, depth), BF16),
            pltpu.VMEM((n, span, depth), BF16),
            pltpu.VMEM(queries.shape, BF16),
            pltpu.VMEM((n, chunk, latent), BF16),
            pltpu.VMEM((n, chunk, latent), BF16),
            pltpu.SemaphoreType.DMA((3,)),
            pltpu.SemaphoreType.DMA,
            pltpu.SemaphoreType.DMA,
            pltpu.SemaphoreType.DMA,
            pltpu.SemaphoreType.DMA,
        ],
        compiler_params=pltpu.CompilerParams(
            collective_id=0, has_side_effects=True, vmem_limit_bytes=40 * 2**20
        ),
        name="attend",
    )(facts, cache, queries, new_keys, value_weight)


class Sum:
    def __init__(self, dims, order, where, me, bufs, recvs, send, recv):
        self.dims, self.order, self.where, self.me = dims, order, where, me
        self.strides = strides_of(dims)
        self.bufs, self.recvs, self.send, self.recv = bufs, recvs, send, recv
        self.flying = []

    def start(self, stage):
        dim = self.order[stage]
        size, at = self.dims[dim], self.where[dim]
        rest = self.bufs[stage].shape[0] // size
        for k in range(1, size):
            target = lax.rem(at + k, size)
            copy = remote(
                self.bufs[stage].at[pl.ds(target * rest, rest)],
                self.recvs[stage].at[k - 1],
                self.send.at[stage, k - 1],
                self.recv.at[stage, k - 1],
                self.me + (target - at) * self.strides[dim],
            )
            copy.start()
            self.flying.append(copy)

    def finish(self, stage):
        for copy in self.flying:
            copy.wait()
        self.flying = []
        dim = self.order[stage]
        size, at = self.dims[dim], self.where[dim]
        rest = self.bufs[stage].shape[0] // size

        def added(j):
            out = self.bufs[stage][at * rest + j].astype(F32)
            for k in range(size - 1):
                out = out + self.recvs[stage][k, j].astype(F32)
            return out

        if stage == len(self.order) - 1:
            return added(0)

        def body(j, carry):
            self.bufs[stage + 1][j] = added(j).astype(BF16)
            return carry

        lax.fori_loop(0, rest, body, 0)
        return None


def spots(dims, order, tail):
    others = dims[:-1]
    out = []
    for flat in range(tail):
        left, coords = flat, []
        for size in reversed(others):
            coords.append(left % size)
            left //= size
        coords = tuple(reversed(coords))
        spot = 0
        for dim in order[1:]:
            spot = spot * dims[dim] + coords[dim]
        out.append(spot)
    return out


def layer_kernel(dims, stages, *refs):
    n = 1
    for size in dims:
        n *= size
    orders = orders_of(dims)
    (mixed, out_weight, hidden, gain, router, picks, gate, up, down, out) = refs[:10]
    rest = list(refs[10:])

    def take(count):
        got = rest[:count]
        del rest[:count]
        return got

    wide, raw, act, activated = take(4)
    state = take(PARTS)
    sums = []
    for _ in range(2):
        sums.append([(take(stages), take(stages)) for _ in range(PARTS)])
    parts = take(PARTS)
    load_sem, sum_send, sum_recv, part_send, part_recv, pass_send, pass_recv = take(7)

    me = lax.axis_index("ep")
    where = place_of(me, dims)
    strides = strides_of(dims)
    width = hidden.shape[1]
    cuts = cuts_of(width)
    tail = n // 2
    rows = hidden.shape[0]
    core = where[-1]

    def runs(p):
        begin, run = cuts[p]
        return [(begin, begin + run), (begin + run, begin + 2 * run)]

    units = gate.shape[1]
    loads = [
        pltpu.make_async_copy(gate, wide.at[:, pl.ds(0, units)], load_sem.at[0]),
        pltpu.make_async_copy(up, wide.at[:, pl.ds(units, units)], load_sem.at[1]),
    ]
    for load in loads:
        load.start()

    barrier = pltpu.get_barrier_semaphore()
    peers = 0
    for dim, size in enumerate(dims):
        for k in range(1, size):
            target = lax.rem(where[dim] + k, size)
            pl.semaphore_signal(
                barrier,
                inc=1,
                device_id={"ep": me + (target - where[dim]) * strides[dim]},
                device_id_type=pl.DeviceIdType.MESH,
            )
            peers += 1
    pl.semaphore_wait(barrier, peers)

    def fill(total, p, c, left, weight):
        place = spots(dims, orders[p], tail)
        begin, run = cuts[p]
        tile = tile_of(run)

        def body(t, carry):
            lo = pl.multiple_of(begin + t * tile, 128)
            hi = pl.multiple_of(begin + run + t * tile, 128)
            at = pl.multiple_of(t * tile, 128)
            rows_left = left[c]
            a = jnp.dot(rows_left, weight[:, pl.ds(lo, tile)], preferred_element_type=F32)
            b = jnp.dot(rows_left, weight[:, pl.ds(hi, tile)], preferred_element_type=F32)
            for i in range(tail):
                both = jnp.concatenate(
                    [a[i * rows : (i + 1) * rows], b[i * rows : (i + 1) * rows]], axis=0
                )
                total.bufs[0][c * tail + place[i], :, pl.ds(at, tile)] = both.astype(BF16)
            return carry

        lax.fori_loop(0, run // tile, body, 0)

    def reduce(which, left, weight):
        total = [
            Sum(
                dims,
                orders[p],
                where,
                me,
                *sums[which][p],
                sum_send.at[which, p],
                sum_recv.at[which, p],
            )
            for p in range(PARTS)
        ]
        for p in range(PARTS):
            fill(total[p], p, 1 - core, left, weight)
            total[p].start(0)
        result = [None] * PARTS
        for stage in range(stages):
            for p in range(PARTS):
                if stage == 0:
                    fill(total[p], p, core, left, weight)
                result[p] = total[p].finish(stage)
                if stage < stages - 1:
                    total[p].start(stage + 1)
        return result

    attended = reduce(0, mixed, out_weight)

    squares = jnp.zeros((rows, 1), F32)
    for p in range(PARTS):
        columns = [hidden[:, lo:hi].astype(F32) for lo, hi in runs(p)]
        value = attended[p] + jnp.concatenate(columns, axis=0)
        state[p][...] = value
        square = jnp.sum(value * value, axis=1, keepdims=True)
        squares = squares + square[:rows] + square[rows:]
    scale = lax.rsqrt(squares / width + 1e-06)
    scale = jnp.concatenate([scale, scale], axis=0)

    mine = []
    for p in range(PARTS):
        spot = 0
        for dim in orders[p]:
            spot = spot * dims[dim] + where[dim]
        mine.append(spot)

    flying = [[] for _ in range(PARTS)]
    passed = [[] for _ in range(PARTS)]
    starts, counts = list(mine), [1] * PARTS

    def send_part(p, stage):
        dim = orders[p][stage]
        size, at = dims[dim], where[dim]
        block = parts[p].at[pl.ds(starts[p], counts[p])]
        for k in range(1, size):
            target = lax.rem(at + k, size)
            copy = remote(
                block,
                block,
                part_send.at[p, stage, k - 1],
                part_recv.at[p, stage, k - 1],
                me + (target - at) * strides[dim],
            )
            copy.start()
            flying[p].append(copy)

    def pass_on(p, begin, count, stage, k):
        block = parts[p].at[pl.ds(begin, count)]
        copy = remote(
            block, block, pass_send.at[p, stage, k], pass_recv.at[p, stage, k], me + 1 - 2 * core
        )
        copy.start()
        passed[p].append(copy)

    def take_part(p, stage):
        for copy in flying[p]:
            copy.wait()
        flying[p].clear()
        dim = orders[p][stage]
        size, at = dims[dim], where[dim]
        base = starts[p] - at * counts[p]
        fresh = [(base + lax.rem(at + k, size) * counts[p], counts[p]) for k in range(1, size)]
        starts[p] = base
        counts[p] = counts[p] * size
        return fresh

    experts = router.shape[0]
    logits = jnp.zeros((rows, experts), F32)
    for p in reversed(range(PARTS)):
        run = cuts[p][1]
        gains = [jnp.broadcast_to(gain[:, lo:hi], (rows, run)) for lo, hi in runs(p)]
        normed = (state[p][...] * scale * jnp.concatenate(gains, axis=0)).astype(BF16)
        parts[p][mine[p], :, pl.ds(0, run)] = normed
        if p > 0:
            send_part(p, stages - 1)
        for i, (lo, hi) in enumerate(runs(p)):
            logits = logits + lax.dot_general(
                normed, router[:, lo:hi], NT, preferred_element_type=F32
            )[i * rows : (i + 1) * rows]
    lane = lax.broadcasted_iota(jnp.int32, (rows, experts), 1)
    wide_lane = lax.broadcasted_iota(jnp.int32, (rows, 128), 1)
    chosen, gates = [], []
    for k in range(picks.shape[1]):
        pick = picks[:, k : k + 1]
        logit = jnp.sum(jnp.where(lane == pick, logits, 0.0), axis=1, keepdims=True)
        gates.append(1.0 / (1.0 + jnp.exp(-logit)))
        chosen.append(pick)
    gate_sum = functools.reduce(jnp.add, gates)
    table = jnp.zeros((rows, 128), F32)
    for pick, score in zip(chosen, gates):
        table = table + jnp.where(wide_lane == pick, ROUTE_SCALE * score / gate_sum, 0.0)
    high = table.astype(BF16).astype(F32)
    share_at = cuts[0][1]
    parts[0][mine[0], :, pl.ds(share_at, 128)] = jnp.concatenate(
        [high, table - high], axis=0
    ).astype(BF16)
    send_part(0, stages - 1)

    turns = list(range(1, PARTS)) + [0]
    for p in turns:
        pass_on(p, mine[p], 1, 0, 0)
    for stage in reversed(range(1, stages)):
        for p in turns:
            fresh = take_part(p, stage)
            if stage > 1:
                send_part(p, stage - 1)
            for k, (begin, count) in enumerate(fresh):
                pass_on(p, begin, count, stage, k)
    for load in loads:
        load.wait()

    def expand(p, c):
        place = spots(dims, orders[p], tail)
        run = cuts[p][1]
        rows_in = parts[p][pl.ds(c * tail, tail), :, pl.ds(0, run)]
        rows_in = rows_in.reshape(tail * 2 * rows, run)
        for i, (lo, hi) in enumerate(runs(p)):
            raw[i] = jnp.dot(rows_in, wide[lo:hi, :], preferred_element_type=F32).reshape(
                tail, 2 * rows, 2 * units
            )
        for j in range(tail):
            block = raw[0, place[j], :rows] + raw[1, place[j], rows:]
            if p == turns[0]:
                act[j] = block
            else:
                act[j] = act[j] + block

    expert = lax.div(me, SPLIT)
    lane = lax.broadcasted_iota(jnp.int32, (rows, 128), 1)
    place = spots(dims, orders[0], tail)

    def activate(c):
        out_rows = []
        for j in range(tail):
            both = act[j]
            g, u = both[:, :units], both[:, units:]
            table = parts[0][c * tail + place[j], :, pl.ds(share_at, 128)].astype(F32)
            share = jnp.where(lane == expert, table[:rows] + table[rows:], 0.0)
            share = jnp.sum(share, axis=1, keepdims=True)
            out_rows.append(g / (1.0 + jnp.exp(-g)) * u * share)
        activated[c] = jnp.concatenate(out_rows, axis=0).astype(BF16)

    for p in turns:
        expand(p, core)
    activate(core)
    for p in turns:
        for copy in passed[p]:
            copy.wait()
        expand(p, 1 - core)
    activate(1 - core)
    combined = reduce(1, activated, down)
    for p in range(PARTS):
        value = state[p][...] + combined[p]
        for i, (lo, hi) in enumerate(runs(p)):
            out[:, lo:hi] = value[i * rows : (i + 1) * rows].astype(BF16)


def layer(dims, mixed, out_weight, hidden, gain, router, picks, gate, up, down):
    orders = orders_of(dims)
    stages = len(dims)
    n = mixed.shape[0] * mixed.shape[1] // hidden.shape[0]
    rows, width = hidden.shape
    cuts = cuts_of(width)
    tail, units = n // 2, gate.shape[1]
    most = max(dims) - 1
    vmem = pl.BlockSpec(memory_space=pltpu.VMEM)
    anywhere = pl.BlockSpec(memory_space=pl.ANY)
    scratch = [
        pltpu.VMEM((width, 2 * units), BF16),
        pltpu.VMEM((2, tail, 2 * rows, 2 * units), F32),
        pltpu.VMEM((tail, rows, 2 * units), F32),
        pltpu.VMEM((2, tail * rows, units), BF16),
    ]
    scratch += [pltpu.VMEM((2 * rows, run), F32) for _, run in cuts]
    for _ in range(2):
        for p in range(PARTS):
            run = cuts[p][1]
            bufs, recvs, left = [], [], n
            for dim in orders[p]:
                size = dims[dim]
                bufs.append(pltpu.VMEM((left, 2 * rows, run), BF16))
                left //= size
                recvs.append(pltpu.VMEM((size - 1, left, 2 * rows, run), BF16))
            scratch += bufs + recvs
    scratch += [
        pltpu.VMEM((n, 2 * rows, cuts[p][1] + (128 if p == 0 else 0)), BF16) for p in range(PARTS)
    ]
    scratch += [
        pltpu.SemaphoreType.DMA((2,)),
        pltpu.SemaphoreType.DMA((2, PARTS, stages, most)),
        pltpu.SemaphoreType.DMA((2, PARTS, stages, most)),
        pltpu.SemaphoreType.DMA((PARTS, stages, most)),
        pltpu.SemaphoreType.DMA((PARTS, stages, most)),
        pltpu.SemaphoreType.DMA((PARTS, stages, most)),
        pltpu.SemaphoreType.DMA((PARTS, stages, most)),
    ]
    return pl.pallas_call(
        functools.partial(layer_kernel, dims, stages),
        out_shape=jax.ShapeDtypeStruct(hidden.shape, BF16),
        in_specs=[vmem, vmem, vmem, vmem, vmem, vmem, anywhere, anywhere, vmem],
        out_specs=vmem,
        scratch_shapes=scratch,
        compiler_params=pltpu.CompilerParams(
            collective_id=1, has_side_effects=True, vmem_limit_bytes=60 * 2**20
        ),
        name="layer",
    )(mixed, out_weight, hidden, gain, router, picks, gate, up, down)


def shards(
    dims,
    cache_src,
    lengths,
    placement,
    queries,
    new_keys,
    hidden,
    latent_value_weight,
    out_weight,
    norm_gain,
    router,
    expert_picks,
    gate_weight,
    up_weight,
    down_weight,
):
    n = lax.axis_size("ep")
    me = lax.axis_index("ep")
    request_ids = jnp.arange(n, dtype=jnp.int32)[None, :]
    slots = jnp.arange(n + 1, dtype=jnp.int32)[:, None]
    named = jnp.where(slots < n, request_ids, lengths[None, :])
    facts = jnp.sum(
        jnp.where(placement[None, :] == jnp.where(slots < n, slots, me), named, 0), axis=1
    ).astype(jnp.int32)
    mixed = attend(
        n,
        facts,
        cache_src.reshape(cache_src.shape[2:]),
        queries.reshape(-1, queries.shape[2]),
        new_keys,
        latent_value_weight,
    )
    return layer(
        dims,
        mixed,
        out_weight,
        hidden,
        norm_gain.reshape(1, -1),
        router,
        expert_picks,
        gate_weight,
        up_weight,
        down_weight,
    )


def solution(mesh):
    in_specs = (
        P(("groups", "ep"), None, None, None, None),
        P("groups"),
        P("groups"),
        P(("groups", "ep"), None, None),
        P(("groups", "ep"), None),
        P(("groups", "ep"), None),
        P("ep", None, None),
        P("ep", None),
        P(),
        P(),
        P(("groups", "ep"), None),
        P(None, "ep"),
        P(None, "ep"),
        P("ep", None),
    )
    out_specs = P(("groups", "ep"), None)
    return jax.shard_map(
        functools.partial(shards, dims_of(mesh)),
        mesh=mesh,
        in_specs=in_specs,
        out_specs=out_specs,
        check_vma=False,
    )
```
